32 devices in a mesh: req: 2 (over x), vocab: 16 (over z, y, core).
Axes of the slice: x: 2, y: 2, z: 4, core: 2. Of those that a mesh axis runs over, the one named last changes fastest.
Arguments:
- hidden: bfloat16 [512, 2304], P(('req', 'vocab'))
- norm_gain: float32 [2304], replicated, may hold values from 0.5 to 1.5
- head_weight: bfloat16 [2304, 16384], P(None, 'vocab')
- targets: int32 [512], P(('req', 'vocab')), may hold values from 0 to 16383
- counts: int32 [32], P(('req', 'vocab')), may hold values from 5 to 10, as said below
Outputs:
- logprob: float32 [512], P(('req', 'vocab'))
- entropy: float32 [512], P(('req', 'vocab'))
The draws below stay inside these ranges and needn't reach their ends.
Inputs may be any that keep to these rules, and one draw needn't show every extreme that they name: The scored slots of a device are its first counts slots; some device holds exactly 10.
All inputs are finite; a program needn't handle non-finite values.
Results may differ from the reference program's by a relative error of at most 0.012.
The reference program's roundings to bfloat16 on the way (of `normed`) count: a program that leaves them out, or rounds other values in their place, can miss the bound.
Values may be sent and summed in bfloat16 or wider, within the bound.
No kernel may reach another device: no remote copies, remote signals or barrier semaphores. Data moves between devices by JAX's collectives and lax.ppermute only.
A program may use at most 64 MiB of HBM per device.

```python
import math
import jax
import jax.numpy as jnp
from jax import lax

D = 2304
SLOTS = 16
CAP = 10
VOCAB = 16384
ROWS = 512


def base_weight(key):
    return jax.random.normal(jax.random.fold_in(key, 11), (D, VOCAB), jnp.float32)


def draw_head_weight(key, part):
    values = base_weight(key)
    return (values * (5000.0 / D)).astype(jnp.bfloat16)


def draw_hidden(key, part):
    noise = jax.random.normal(jax.random.fold_in(key, 21), (ROWS, D), jnp.float32)
    row_scale = jnp.exp(jax.random.uniform(jax.random.fold_in(key, 22), (ROWS, 1), jnp.float32) * 2.302585)
    col_scale = jnp.exp(jax.random.uniform(jax.random.fold_in(key, 23), (1, D), jnp.float32) * 2.302585)
    values = noise * row_scale * col_scale
    weight = base_weight(key)
    first = jax.random.randint(jax.random.fold_in(key, 24), (ROWS,), 0, VOCAB)
    second = jax.random.randint(jax.random.fold_in(key, 25), (ROWS,), 0, VOCAB)
    picked = jax.random.randint(jax.random.fold_in(key, 26), (ROWS,), 0, 8) == 0
    power = jax.random.randint(jax.random.fold_in(key, 27), (ROWS,), -2, 3).astype(jnp.float32)
    strength = jnp.exp(power * 0.693147)
    aligned = strength[:, None] * (weight[:, first].T + 0.99 * weight[:, second].T) + noise
    values = jnp.where(picked[:, None], aligned, values)
    return values.astype(jnp.bfloat16)


def draw_counts(key, part):
    owners = ROWS // SLOTS
    drawn = jax.random.randint(jax.random.fold_in(key, 31), (owners,), CAP // 2, CAP + 1)
    fullest = jax.random.randint(jax.random.fold_in(key, 32), (), 0, owners)
    return drawn.at[fullest].set(CAP).astype(jnp.int32)


def plant(result, own_key, low, largest):
    dims = result.shape
    index_at = [jax.random.randint(jax.random.fold_in(own_key, axis), (), 0, dims[axis]) for axis in range(len(dims))]
    result = result.at[tuple(index_at)].set(low)
    longest = dims.index(max(dims))
    index_at[longest] = (index_at[longest] + 1) % dims[longest]
    return result.at[tuple(index_at)].set(largest)


def setup_inputs(seed: int = 0) -> dict:
    keys = jax.random.split(jax.random.key(seed), 6)
    return {
        "hidden": draw_hidden(jax.random.fold_in(keys[5], 71), 0),
        "norm_gain": jnp.clip(1.0 + 0.1 * jax.random.normal(keys[1], (D,), jnp.float32), 0.5, 1.5),
        "head_weight": draw_head_weight(jax.random.fold_in(keys[5], 71), 0),
        "targets": plant(jax.random.randint(keys[3], (ROWS,), 0, VOCAB), jax.random.fold_in(keys[3], 1), 0, VOCAB - 1).astype(jnp.int32),
        "counts": draw_counts(jax.random.fold_in(keys[5], 71), 0),
    }


logit_scale = 256.0 / 2304.0

def reference(hidden, norm_gain, head_weight, targets, counts):
    values = hidden.astype(jnp.float32)
    square_mean = lax.optimization_barrier(jnp.mean(values * values, axis=1, keepdims=True))
    normed = (values * lax.rsqrt(square_mean + 1e-05) * norm_gain[None, :]).astype(jnp.bfloat16)
    block = math.gcd(ROWS, 512)

    def block_stats(pair):
        rows_blk, target_blk = pair
        logits = jnp.dot(rows_blk, head_weight, preferred_element_type=jnp.float32) * logit_scale
        peak = lax.optimization_barrier(jnp.max(logits, axis=1))
        weights = jnp.exp(logits - peak[:, None])
        total = lax.optimization_barrier(jnp.sum(weights, axis=1))
        moment = lax.optimization_barrier(jnp.sum(weights * logits, axis=1))
        chosen = jnp.take_along_axis(logits, target_blk[:, None], axis=1)[:, 0]
        return (chosen - peak - jnp.log(total), peak + jnp.log(total) - moment / total)
    logp, entr = lax.map(block_stats, (normed.reshape(ROWS // block, block, D), targets.reshape(ROWS // block, block)))
    logp = logp.reshape(ROWS)
    entr = entr.reshape(ROWS)
    slot_index = jnp.arange(ROWS, dtype=jnp.int32)
    scored = slot_index % SLOTS < jnp.repeat(counts, SLOTS)
    logprob = jnp.where(scored, logp, jnp.float32(0.0))
    entropy = jnp.where(scored, entr, jnp.float32(0.0))
    return (logprob, entropy)
```

```python
import jax
import jax.numpy as jnp
from jax import lax
from jax.sharding import PartitionSpec as P

logit_scale = 256.0 / 2304.0


def gather_masks(n):
    if n == 16:
        return [[5, 8, 13], [3], [1]]
    steps, bit = [], n // 2
    while bit:
        steps.append([bit])
        bit //= 2
    return steps


def swap(block, mask, n):
    return lax.ppermute(block, "vocab", [(i, i ^ mask) for i in range(n)])


def gather(block, n):
    blocks, owners = [block], [0]
    for masks in gather_masks(n):
        if len(blocks) == n // 2:
            whole = jnp.concatenate([jnp.stack(blocks)])
            got = swap(whole, masks[0], n)
            return jnp.concatenate([whole, got]), owners + [o ^ masks[0] for o in owners]
        got = [swap(b, mask, n) for mask in masks for b in blocks]
        owners = owners + [o ^ mask for mask in masks for o in owners]
        blocks = blocks + got
    return jnp.stack(blocks), owners


def on_device(n, hidden, norm_gain, head_weight, targets, counts):
    slots, width = hidden.shape
    vocab_dev = head_weight.shape[1]
    values = hidden.astype(jnp.float32)
    square_mean = jnp.mean(values * values, axis=1, keepdims=True)
    normed = (values * lax.rsqrt(square_mean + 1e-05) * norm_gain[None, :]).astype(jnp.bfloat16)
    ids = jnp.stack([targets // 256, targets % 256], axis=1).astype(jnp.bfloat16)
    payload = jnp.concatenate([normed, jnp.pad(ids, ((0, 0), (0, 126)))], axis=1)
    blocks, owners = gather(payload, n)
    rows = blocks.reshape(n * slots, width + 128)
    gathered = rows[:, :width]
    ids = rows[:, width:width + 2].astype(jnp.int32)
    wanted = ids[:, 0] * 256 + ids[:, 1]
    position = lax.axis_index("vocab")
    logits = jnp.dot(gathered, head_weight, preferred_element_type=jnp.float32) * logit_scale
    local_peak = jnp.max(logits, axis=1)
    weights = jnp.exp(logits - local_peak[:, None])
    local_total = jnp.sum(weights, axis=1)
    local_moment = jnp.sum(weights * logits, axis=1)
    columns = lax.broadcasted_iota(jnp.int32, logits.shape, 1)
    hits = columns == (wanted - position * vocab_dev)[:, None]
    local_chosen = jnp.sum(jnp.where(hits, logits, jnp.float32(0.0)), axis=1)
    stats = jnp.stack([local_peak, local_total, local_moment, local_chosen]).reshape(4, n, slots)
    owner_of = jnp.array(owners, jnp.int32) ^ position
    one_hot = jnp.arange(n, dtype=jnp.int32)[:, None] == owner_of[None, :]
    placed = jnp.sum(jnp.where(one_hot[:, :, None, None], stats.transpose(1, 0, 2)[None], 0.0), axis=1)
    back = lax.all_to_all(placed, "vocab", 0, 0, tiled=True)
    peaks, totals, moments, chosens = back[:, 0], back[:, 1], back[:, 2], back[:, 3]
    peak = jnp.max(peaks, axis=0)
    factor = jnp.exp(peaks - peak[None])
    total = jnp.sum(totals * factor, axis=0)
    moment = jnp.sum(moments * factor, axis=0)
    chosen = jnp.sum(chosens, axis=0)
    log_total = jnp.log(total)
    scored = jnp.arange(slots, dtype=jnp.int32) < counts[0]
    logprob = jnp.where(scored, chosen - peak - log_total, jnp.float32(0.0))
    entropy = jnp.where(scored, peak + log_total - moment / total, jnp.float32(0.0))
    return (logprob, entropy)


def solution(mesh):
    n = mesh.shape["vocab"]
    in_specs = (
        P(("req", "vocab"), None),
        P(),
        P(None, "vocab"),
        P(("req", "vocab")),
        P(("req", "vocab")),
    )
    out_specs = (P(("req", "vocab")), P(("req", "vocab")))

    def step(*args):
        return on_device(n, *args)

    return jax.shard_map(step, mesh=mesh, in_specs=in_specs, out_specs=out_specs, check_vma=False)
```

```python
import functools

import jax
import jax.numpy as jnp
from jax import lax
from jax.experimental import pallas as pl
from jax.experimental.pallas import tpu as pltpu
from jax.sharding import PartitionSpec as P

logit_scale = 256.0 / 2304.0
CAP = 10
HEAD = 8
TAIL = CAP - HEAD
LANES = 128
PER_TILE = HEAD // TAIL


def gather_masks(n):
    if n == 16:
        return [[5, 8, 13], [3], [1]]
    steps, bit = [], n // 2
    while bit:
        steps.append([bit])
        bit //= 2
    return steps


def swap(block, mask, n):
    return lax.ppermute(block, "vocab", [(i, i ^ mask) for i in range(n)])


def strip_at(chunks, c):
    tile, place = divmod(c, PER_TILE)
    return slice(TAIL * place, TAIL * place + TAIL), slice((chunks + tile) * LANES, (chunks + tile + 1) * LANES)


def front_kernel(hidden_ref, gain_ref, targets_ref, block_ref):
    slots, width = hidden_ref.shape
    chunks = width // LANES
    values = hidden_ref[...].astype(jnp.float32)
    square_mean = jnp.sum(values * values, axis=1, keepdims=True) * (1.0 / width)
    gain = gain_ref[...].reshape(1, width)
    normed = (values * lax.rsqrt(square_mean + 1e-05) * gain).astype(jnp.bfloat16)
    block_ref[:, :width] = normed[:HEAD]
    for c in range(chunks):
        rows, columns = strip_at(chunks, c)
        block_ref[rows, columns] = normed[HEAD:CAP, c * LANES:(c + 1) * LANES]
    ids = jnp.broadcast_to(targets_ref[...].reshape(1, slots), (TAIL, slots))
    part = lax.broadcasted_iota(jnp.int32, ids.shape, 0)
    ids = jnp.where(part == 0, lax.shift_right_logical(ids, 8), ids & 255)
    rows, columns = strip_at(chunks, chunks)
    block_ref[rows, columns.start:columns.start + slots] = ids.astype(jnp.float32).astype(jnp.bfloat16)


def front(hidden, gain, targets):
    chunks = hidden.shape[1] // LANES
    tiles = chunks + -(-(chunks + 1) // PER_TILE)
    return pl.pallas_call(
        front_kernel,
        out_shape=jax.ShapeDtypeStruct((HEAD, tiles * LANES), jnp.bfloat16),
        in_specs=[pl.BlockSpec(memory_space=pltpu.VMEM)] * 3,
        out_specs=pl.BlockSpec(memory_space=pltpu.VMEM),
        name="norm_and_pack",
    )(hidden, gain, targets)


def stats_kernel(owners, n_cols, near_ref, far_ref, weight_ref, out_ref, rows_ref, logits_ref):
    n = len(owners)
    half = n // 2
    width, vocab_dev = weight_ref.shape
    chunks = width // LANES
    me = lax.axis_index("vocab")
    start = me * vocab_dev
    base = n * HEAD
    lane = lax.broadcasted_iota(jnp.int32, (HEAD, LANES), 1)
    sub = lax.broadcasted_iota(jnp.int32, (HEAD, LANES), 0)
    id_rows, id_columns = strip_at(chunks, chunks)
    head_ids, tail_ids = [], []
    for b in range(n):
        ref, at = (near_ref, b) if b < half else (far_ref, b - half)
        rows_ref[b * HEAD:(b + 1) * HEAD, :] = ref[at, :, :width]
        for c in range(chunks):
            r, k = strip_at(chunks, c)
            rows_ref[base + TAIL * b:base + TAIL * (b + 1), c * LANES:(c + 1) * LANES] = ref[at, r, k]
        ids = ref[at, id_rows, id_columns].astype(jnp.float32)
        ids = ids[0:1] * 256.0 + ids[1:2]
        ids = jnp.broadcast_to(ids, (HEAD, LANES))
        head_ids.append(jnp.sum(jnp.where(lane == sub, ids, 0.0), axis=1, keepdims=True))
        tail_ids.append(jnp.sum(jnp.where((lane == sub + HEAD)[:TAIL], ids[:TAIL], 0.0), axis=1, keepdims=True))
    wanted = jnp.concatenate(head_ids + tail_ids, axis=0).astype(jnp.int32) - start
    m = n * CAP
    peak = None
    for j in range(0, vocab_dev, n_cols):
        z = jnp.dot(rows_ref[...], weight_ref[:, j:j + n_cols], preferred_element_type=jnp.float32) * logit_scale
        logits_ref[:, j:j + n_cols] = z
        top = z[:, :LANES]
        for k in range(LANES, n_cols, LANES):
            top = jnp.maximum(top, z[:, k:k + LANES])
        peak = top if peak is None else jnp.maximum(peak, top)
    peak = jnp.max(peak, axis=1, keepdims=True)
    total = jnp.zeros((m, LANES), jnp.float32)
    moment = jnp.zeros((m, LANES), jnp.float32)
    chosen = jnp.zeros((m, LANES), jnp.float32)
    column = lax.broadcasted_iota(jnp.int32, (m, LANES), 1)
    for j in range(0, vocab_dev, LANES):
        z = logits_ref[:, j:j + LANES]
        e = jnp.exp(z - peak)
        total += e
        moment += e * z
        chosen += jnp.where(column == wanted - j, z, 0.0)
    total = jnp.sum(total, axis=1, keepdims=True)
    moment = jnp.sum(moment, axis=1, keepdims=True)
    chosen = jnp.sum(chosen, axis=1, keepdims=True)
    table = jnp.where(column == 0, peak, jnp.where(column == 1, total, jnp.where(column == 2, moment, chosen)))
    for b in range(n):
        to = me ^ owners[b]
        out_ref[to, :HEAD] = table[b * HEAD:(b + 1) * HEAD]
        out_ref[to, HEAD:CAP] = table[base + TAIL * b:base + TAIL * (b + 1)]


def row_stats(owners, near, far, weight):
    n = len(owners)
    width, vocab_dev = weight.shape
    return pl.pallas_call(
        functools.partial(stats_kernel, owners, 256),
        out_shape=jax.ShapeDtypeStruct((n, 16, LANES), jnp.float32),
        in_specs=[pl.BlockSpec(memory_space=pltpu.VMEM)] * 3,
        out_specs=pl.BlockSpec(memory_space=pltpu.VMEM),
        scratch_shapes=[
            pltpu.VMEM((n * CAP, width), jnp.bfloat16),
            pltpu.VMEM((n * CAP, vocab_dev), jnp.float32),
        ],
        compiler_params=pltpu.CompilerParams(vmem_limit_bytes=32 * 1024 * 1024),
        name="row_stats",
    )(near, far, weight)


def on_device(n, hidden, norm_gain, head_weight, targets, counts):
    slots = hidden.shape[0]
    block = front(hidden, norm_gain, targets)
    blocks, owners = [block], [0]
    *steps, last = gather_masks(n)
    for masks in steps:
        got = [swap(b, mask, n) for mask in masks for b in blocks]
        owners = owners + [o ^ mask for mask in masks for o in owners]
        blocks = blocks + got
    near = jnp.stack(blocks)
    far = swap(near, last[0], n)
    owners = owners + [o ^ last[0] for o in owners]
    stats = row_stats(tuple(owners), near, far, head_weight)
    back = lax.all_to_all(stats, "vocab", 0, 0, tiled=True)
    peaks, totals, moments, chosens = (back[:, :slots, k] for k in range(4))
    scored = jnp.arange(slots, dtype=jnp.int32) < counts[0]
    peak = jnp.max(peaks, axis=0)
    factor = jnp.exp(peaks - peak[None])
    total = jnp.sum(totals * factor, axis=0)
    moment = jnp.sum(moments * factor, axis=0)
    chosen = jnp.sum(chosens, axis=0)
    log_total = jnp.log(total)
    logprob = jnp.where(scored, chosen - peak - log_total, jnp.float32(0.0))
    entropy = jnp.where(scored, peak + log_total - moment / total, jnp.float32(0.0))
    return (logprob, entropy)


def solution(mesh):
    n = mesh.shape["vocab"]
    in_specs = (
        P(("req", "vocab"), None),
        P(),
        P(None, "vocab"),
        P(("req", "vocab")),
        P(("req", "vocab")),
    )
    out_specs = (P(("req", "vocab")), P(("req", "vocab")))

    def step(*args):
        return on_device(n, *args)

    return jax.shard_map(step, mesh=mesh, in_specs=in_specs, out_specs=out_specs, check_vma=False)
```

```python
import functools

import jax
import jax.numpy as jnp
from jax import lax
from jax.experimental import pallas as pl
from jax.experimental.pallas import tpu as pltpu
from jax.sharding import PartitionSpec as P

logit_scale = 256.0 / 2304.0
CAP = 10
HEAD = 8
TAIL = CAP - HEAD
LANES = 128
PER_TILE = HEAD // TAIL
FIELD = 16
VMEM = pl.BlockSpec(memory_space=pltpu.VMEM)
ANY = pl.BlockSpec(memory_space=pl.ANY)
MIB = 1024 * 1024


def gather_masks(n):
    if n == 16:
        return [[8, 5, 13], [3], [1]]
    steps, bit = [], n // 2
    while bit:
        steps.append([bit])
        bit //= 2
    return steps


def swap(block, mask, n):
    return lax.ppermute(block, "vocab", [(i, i ^ mask) for i in range(n)])


def in_hbm(array):
    return pltpu.with_memory_space_constraint(array, pltpu.HBM)


def strip_at(chunks, c):
    tile, place = divmod(c, PER_TILE)
    return slice(TAIL * place, TAIL * place + TAIL), slice((chunks + tile) * LANES, (chunks + tile + 1) * LANES)


def front_kernel(
    hidden_hbm, gain_hbm, targets_hbm, counts_ref, block_ref, scored_ref, hidden_ref, gain_ref, targets_ref, sems
):
    copies = [
        pltpu.make_async_copy(source, target, sems.at[i])
        for i, (source, target) in enumerate(
            [(hidden_hbm, hidden_ref), (gain_hbm, gain_ref), (targets_hbm, targets_ref)]
        )
    ]
    for copy in copies:
        copy.start()
    for copy in copies:
        copy.wait()
    slots, width = hidden_ref.shape
    chunks = width // LANES + 1
    values = hidden_ref[...].astype(jnp.float32)
    square_mean = jnp.sum(values * values, axis=1, keepdims=True) * (1.0 / width)
    gain = gain_ref[...].reshape(1, width)
    normed = (values * lax.rsqrt(square_mean + 1e-05) * gain).astype(jnp.bfloat16)
    lane = lax.broadcasted_iota(jnp.int32, (slots, LANES), 1)
    sub = lax.broadcasted_iota(jnp.int32, (slots, LANES), 0)
    ids = jnp.broadcast_to(targets_ref[...].reshape(1, slots), (slots, slots))
    own = lax.broadcasted_iota(jnp.int32, (slots, slots), 0) == lax.broadcasted_iota(jnp.int32, (slots, slots), 1)
    ids = jnp.sum(jnp.where(own, ids, 0).astype(jnp.float32), axis=1, keepdims=True).astype(jnp.int32)
    ids = jnp.where(lane == 0, lax.shift_right_logical(ids, 8), jnp.where(lane == 1, ids & 255, 0))
    ids = ids.astype(jnp.float32).astype(jnp.bfloat16)
    block_ref[:, :width] = normed[:HEAD]
    block_ref[:, width:width + LANES] = ids[:HEAD]
    for c in range(chunks):
        rows, columns = strip_at(chunks, c)
        chunk = ids if c == chunks - 1 else normed[:, c * LANES:(c + 1) * LANES]
        block_ref[rows, columns] = chunk[HEAD:CAP]
    scored_ref[...] = (lane[:HEAD] < counts_ref[0]).astype(jnp.float32)


def front(hidden, gain, targets, counts):
    slots, width = hidden.shape
    chunks = width // LANES + 1
    tiles = chunks + -(-chunks // PER_TILE)
    return pl.pallas_call(
        front_kernel,
        out_shape=(pltpu.VMEM((HEAD, tiles * LANES), jnp.bfloat16), pltpu.VMEM((HEAD, LANES), jnp.float32)),
        in_specs=[ANY] * 3 + [pl.BlockSpec(memory_space=pltpu.SMEM)],
        out_specs=[VMEM] * 2,
        scratch_shapes=[
            pltpu.VMEM(hidden.shape, hidden.dtype),
            pltpu.VMEM(gain.shape, gain.dtype),
            pltpu.VMEM(targets.shape, targets.dtype),
            pltpu.SemaphoreType.DMA((3,)),
        ],
        compiler_params=pltpu.CompilerParams(vmem_limit_bytes=4 * MIB),
        name="norm_and_pack",
    )(in_hbm(hidden), in_hbm(gain), in_hbm(targets), counts)


def fetch_kernel(after_ref, weight_ref, out_ref, sems):
    del after_ref
    parts = sems.shape[0]
    rows = weight_ref.shape[0] // parts
    copies = [
        pltpu.make_async_copy(weight_ref.at[pl.ds(i * rows, rows)], out_ref.at[pl.ds(i * rows, rows)], sems.at[i])
        for i in range(parts)
    ]
    for copy in copies:
        copy.start()
    for copy in copies:
        copy.wait()


def fetch(after, weight):
    return pl.pallas_call(
        fetch_kernel,
        out_shape=pltpu.VMEM(weight.shape, weight.dtype),
        in_specs=[ANY] * 2,
        out_specs=VMEM,
        scratch_shapes=[pltpu.SemaphoreType.DMA((8,))],
        cost_estimate=pl.CostEstimate(flops=0, bytes_accessed=2 * weight.size, transcendentals=0),
        compiler_params=pltpu.CompilerParams(vmem_limit_bytes=MIB),
        name="fetch_weights",
    )(after, in_hbm(weight))


def unpack_kernel(*refs):
    *blocks, out_ref = refs
    base = len(blocks) * HEAD
    chunks = out_ref.shape[1] // LANES
    for b, ref in enumerate(blocks):
        out_ref[b * HEAD:(b + 1) * HEAD, :] = ref[:, :chunks * LANES]
        for c in range(chunks):
            rows, columns = strip_at(chunks, c)
            out_ref[base + TAIL * b:base + TAIL * (b + 1), c * LANES:(c + 1) * LANES] = ref[rows, columns]


def unpack(blocks, width):
    return pl.pallas_call(
        unpack_kernel,
        out_shape=pltpu.VMEM((len(blocks) * CAP, width + LANES), jnp.bfloat16),
        in_specs=[VMEM] * len(blocks),
        out_specs=VMEM,
        compiler_params=pltpu.CompilerParams(vmem_limit_bytes=4 * MIB),
        name="unpack",
    )(*blocks)


def stats_kernel(owners, n_cols, near_ref, far_ref, weight_ref, out_ref, logits_ref):
    n = len(owners)
    half = n // 2
    width, vocab_dev = weight_ref.shape
    m = n * CAP
    me = lax.axis_index("vocab")
    rows = jnp.concatenate([near_ref[:, :width], far_ref[:, :width]], axis=0)
    ids = jnp.concatenate([near_ref[:, width:], far_ref[:, width:]], axis=0).astype(jnp.float32)
    wanted = (ids[:, 0:1] * 256.0 + ids[:, 1:2]).astype(jnp.int32) - me * vocab_dev
    peak = None
    for j in range(0, vocab_dev, n_cols):
        z = jnp.dot(rows, weight_ref[:, j:j + n_cols], preferred_element_type=jnp.float32) * logit_scale
        logits_ref[:, j:j + n_cols] = z
        for k in range(0, n_cols, LANES):
            part = z[:, k:k + LANES]
            peak = part if peak is None else jnp.maximum(peak, part)
    peak = jnp.max(peak, axis=1, keepdims=True)
    total = jnp.zeros((m, LANES), jnp.float32)
    moment = jnp.zeros((m, LANES), jnp.float32)
    chosen = jnp.zeros((m, LANES), jnp.float32)
    column = lax.broadcasted_iota(jnp.int32, (m, LANES), 1)
    for j in range(0, vocab_dev, LANES):
        z = logits_ref[:, j:j + LANES]
        e = jnp.exp(z - peak)
        total += e
        moment += e * z
        chosen += jnp.where(column == wanted - j, z, 0.0)
    total = jnp.sum(total, axis=1, keepdims=True)
    moment = jnp.sum(moment, axis=1, keepdims=True)
    chosen = jnp.sum(chosen, axis=1, keepdims=True)
    field = lax.shift_right_logical(column, 4)
    table = jnp.where(field == 0, peak, jnp.where(field == 1, total, jnp.where(field == 2, moment, chosen)))
    lane = lax.broadcasted_iota(jnp.int32, (HEAD, LANES), 1) & (FIELD - 1)
    sub = lax.broadcasted_iota(jnp.int32, (HEAD, LANES), 0)
    tail_mask = lane == HEAD + (sub & (TAIL - 1))
    for b in range(n):
        at = (b // half) * half * CAP
        k = b % half
        head = jnp.where(lane == sub, table[at + k * HEAD:at + (k + 1) * HEAD], 0.0)
        first = at + half * HEAD + k * TAIL
        tile, place = first // HEAD * HEAD, first % HEAD
        inside = tail_mask & (sub >= place) & (sub < place + TAIL)
        line = head + jnp.where(inside, table[tile:tile + HEAD], 0.0)
        out_ref[pl.ds(me ^ owners[b], 1), :] = jnp.sum(line, axis=0, keepdims=True)


def row_stats(owners, near, far, weight):
    n = len(owners)
    width, vocab_dev = weight.shape
    return pl.pallas_call(
        functools.partial(stats_kernel, owners, 256),
        out_shape=pltpu.VMEM((n, LANES), jnp.float32),
        in_specs=[VMEM] * 3,
        out_specs=VMEM,
        scratch_shapes=[pltpu.VMEM((n * CAP, vocab_dev), jnp.float32)],
        compiler_params=pltpu.CompilerParams(vmem_limit_bytes=16 * MIB),
        name="row_stats",
    )(near, far, weight)


def finish_kernel(lines_ref, scored_ref, logprob_ref, entropy_ref):
    slots = logprob_ref.shape[0]
    lines = lines_ref[...]
    peak = jnp.max(lines, axis=0, keepdims=True)
    factor = jnp.exp(lines - peak)

    def field(k):
        return pltpu.roll(lines, LANES - FIELD * k, 1)

    total = jnp.sum(field(1) * factor, axis=0, keepdims=True)
    moment = jnp.sum(field(2) * factor, axis=0, keepdims=True)
    chosen = jnp.sum(field(3), axis=0, keepdims=True)
    log_total = jnp.log(total)
    scored = scored_ref[0:1] > 0.0
    logprob = jnp.where(scored, chosen - peak - log_total, 0.0)
    entropy = jnp.where(scored, peak + log_total - moment / total, 0.0)
    logprob_ref[...] = logprob[0, :slots]
    entropy_ref[...] = entropy[0, :slots]


def finish(lines, scored, slots):
    return pl.pallas_call(
        finish_kernel,
        out_shape=(jax.ShapeDtypeStruct((slots,), jnp.float32),) * 2,
        in_specs=[VMEM] * 2,
        out_specs=[VMEM] * 2,
        compiler_params=pltpu.CompilerParams(vmem_limit_bytes=4 * MIB),
        name="finish",
    )(lines, scored)


def on_device(n, hidden, norm_gain, head_weight, targets, counts):
    slots, width = hidden.shape
    block, scored = front(hidden, norm_gain, targets, counts)
    blocks, owners = [block], [0]
    *steps, last = gather_masks(n)
    for masks in steps:
        got = [swap(b, mask, n) for mask in masks for b in blocks]
        owners = owners + [o ^ mask for mask in masks for o in owners]
        blocks = blocks + got
    weight = fetch(blocks[len(blocks) // 2 - 1], head_weight)
    weight, *blocks = lax.optimization_barrier((weight, *blocks))
    near = unpack(blocks, width)
    far = swap(near, last[0], n)
    owners = owners + [o ^ last[0] for o in owners]
    lines = row_stats(tuple(owners), near, far, weight)
    lines = lax.all_to_all(lines, "vocab", 0, 0, tiled=True)
    return finish(lines, scored, slots)


def solution(mesh):
    n = mesh.shape["vocab"]
    in_specs = (
        P(("req", "vocab"), None),
        P(),
        P(None, "vocab"),
        P(("req", "vocab")),
        P(("req", "vocab")),
    )
    out_specs = (P(("req", "vocab")), P(("req", "vocab")))

    def step(*args):
        return on_device(n, *args)

    return jax.shard_map(step, mesh=mesh, in_specs=in_specs, out_specs=out_specs, check_vma=False)
```

```python
import functools

import jax
import jax.numpy as jnp
from jax import lax
from jax.experimental import pallas as pl
from jax.experimental.pallas import tpu as pltpu
from jax.sharding import PartitionSpec as P

logit_scale = 256.0 / 2304.0
CAP = 10
HEAD = 8
TAIL = CAP - HEAD
LANES = 128
PER_TILE = HEAD // TAIL
FIELD = 16
VMEM = pl.BlockSpec(memory_space=pltpu.VMEM)
ANY = pl.BlockSpec(memory_space=pl.ANY)
MIB = 1024 * 1024
N_COLS = 256
FETCH = {"all": (0, 1024)}
MASKS = [5, 8, 13]


def gather_masks(n):
    if n == 16:
        return [MASKS, [3], [1]]
    steps, bit = [], n // 2
    while bit:
        steps.append([bit])
        bit //= 2
    return steps


def swap(block, mask, n):
    return lax.ppermute(block, "vocab", [(i, i ^ mask) for i in range(n)])


def in_hbm(array):
    return pltpu.with_memory_space_constraint(array, pltpu.HBM)


def strip_at(chunks, c):
    tile, place = divmod(c, PER_TILE)
    return slice(TAIL * place, TAIL * place + TAIL), slice((chunks + tile) * LANES, (chunks + tile + 1) * LANES)


def front_kernel(
    hidden_hbm, gain_hbm, targets_hbm, block_ref, hidden_ref, gain_ref, targets_ref, sems
):
    copies = [
        pltpu.make_async_copy(source, target, sems.at[i])
        for i, (source, target) in enumerate(
            [(hidden_hbm, hidden_ref), (gain_hbm, gain_ref), (targets_hbm, targets_ref)]
        )
    ]
    for copy in copies:
        copy.start()
    for copy in copies:
        copy.wait()
    slots, width = hidden_ref.shape
    chunks = width // LANES + 1
    values = hidden_ref[...].astype(jnp.float32)
    square_mean = jnp.sum(values * values, axis=1, keepdims=True) * (1.0 / width)
    gain = gain_ref[...].reshape(1, width)
    normed = (values * lax.rsqrt(square_mean + 1e-05) * gain).astype(jnp.bfloat16)
    lane = lax.broadcasted_iota(jnp.int32, (slots, LANES), 1)
    sub = lax.broadcasted_iota(jnp.int32, (slots, LANES), 0)
    ids = jnp.broadcast_to(targets_ref[...].reshape(1, slots), (slots, slots))
    own = lax.broadcasted_iota(jnp.int32, (slots, slots), 0) == lax.broadcasted_iota(jnp.int32, (slots, slots), 1)
    ids = jnp.sum(jnp.where(own, ids, 0).astype(jnp.float32), axis=1, keepdims=True).astype(jnp.int32)
    ids = jnp.where(lane == 0, lax.shift_right_logical(ids, 8), jnp.where(lane == 1, ids & 255, 0))
    ids = ids.astype(jnp.float32).astype(jnp.bfloat16)
    block_ref[:, :width] = normed[:HEAD]
    block_ref[:, width:width + LANES] = ids[:HEAD]
    for c in range(chunks):
        rows, columns = strip_at(chunks, c)
        chunk = ids if c == chunks - 1 else normed[:, c * LANES:(c + 1) * LANES]
        block_ref[rows, columns] = chunk[HEAD:CAP]


def front(hidden, gain, targets):
    slots, width = hidden.shape
    chunks = width // LANES + 1
    tiles = chunks + -(-chunks // PER_TILE)
    return pl.pallas_call(
        front_kernel,
        out_shape=pltpu.VMEM((HEAD, tiles * LANES), jnp.bfloat16),
        in_specs=[ANY] * 3,
        out_specs=VMEM,
        scratch_shapes=[
            pltpu.VMEM(hidden.shape, hidden.dtype),
            pltpu.VMEM(gain.shape, gain.dtype),
            pltpu.VMEM(targets.shape, targets.dtype),
            pltpu.SemaphoreType.DMA((3,)),
        ],
        compiler_params=pltpu.CompilerParams(vmem_limit_bytes=4 * MIB),
        name="norm_and_pack",
    )(in_hbm(hidden), in_hbm(gain), in_hbm(targets))


def fetch_kernel(first, after_ref, weight_ref, out_ref, sem):
    del after_ref
    copy = pltpu.make_async_copy(weight_ref.at[:, pl.ds(first, out_ref.shape[1])], out_ref, sem)
    copy.start()
    copy.wait()


def fetch(after, weight, first, last):
    shape = (weight.shape[0], last - first)
    return pl.pallas_call(
        functools.partial(fetch_kernel, first),
        out_shape=pltpu.VMEM(shape, weight.dtype),
        in_specs=[ANY] * 2,
        out_specs=VMEM,
        scratch_shapes=[pltpu.SemaphoreType.DMA],
        cost_estimate=pl.CostEstimate(flops=0, bytes_accessed=2 * shape[0] * shape[1], transcendentals=0),
        compiler_params=pltpu.CompilerParams(vmem_limit_bytes=MIB),
        name="fetch_weights",
    )(after, in_hbm(weight))


def unpack_kernel(*refs):
    *blocks, out_ref = refs
    base = len(blocks) * HEAD
    chunks = out_ref.shape[1] // LANES
    for b, ref in enumerate(blocks):
        out_ref[b * HEAD:(b + 1) * HEAD, :] = ref[:, :chunks * LANES]
        for c in range(chunks):
            rows, columns = strip_at(chunks, c)
            out_ref[base + TAIL * b:base + TAIL * (b + 1), c * LANES:(c + 1) * LANES] = ref[rows, columns]


def unpack(blocks, width):
    return pl.pallas_call(
        unpack_kernel,
        out_shape=pltpu.VMEM((len(blocks) * CAP, width + LANES), jnp.bfloat16),
        in_specs=[VMEM] * len(blocks),
        out_specs=VMEM,
        compiler_params=pltpu.CompilerParams(vmem_limit_bytes=4 * MIB),
        name="unpack",
    )(*blocks)


def stats_kernel(owners, near_ref, far_ref, *refs):
    *weight_refs, out_ref, logits_ref = refs
    n = len(owners)
    half = n // 2
    width = near_ref.shape[1] - LANES
    vocab_dev = logits_ref.shape[1]
    m = n * CAP
    me = lax.axis_index("vocab")
    rows = jnp.concatenate([near_ref[:, :width], far_ref[:, :width]], axis=0)
    ids = jnp.concatenate([near_ref[:, width:], far_ref[:, width:]], axis=0).astype(jnp.float32)
    wanted = (ids[:, 0:1] * 256.0 + ids[:, 1:2]).astype(jnp.int32) - me * vocab_dev
    peak, first = None, 0
    for ref in weight_refs:
        for j in range(0, ref.shape[1], N_COLS):
            z = jnp.dot(rows, ref[:, j:j + N_COLS], preferred_element_type=jnp.float32) * logit_scale
            logits_ref[:, first:first + N_COLS] = z
            first += N_COLS
            for k in range(0, N_COLS, LANES):
                part = z[:, k:k + LANES]
                peak = part if peak is None else jnp.maximum(peak, part)
    peak = jnp.max(peak, axis=1, keepdims=True)
    total = jnp.zeros((m, LANES), jnp.float32)
    moment = jnp.zeros((m, LANES), jnp.float32)
    chosen = jnp.zeros((m, LANES), jnp.float32)
    column = lax.broadcasted_iota(jnp.int32, (m, LANES), 1)
    for j in range(0, vocab_dev, LANES):
        z = logits_ref[:, j:j + LANES]
        e = jnp.exp(z - peak)
        total += e
        moment += e * z
        chosen += jnp.where(column == wanted - j, z, 0.0)
    total = jnp.sum(total, axis=1, keepdims=True)
    moment = jnp.sum(moment, axis=1, keepdims=True)
    chosen = jnp.sum(chosen, axis=1, keepdims=True)
    field = lax.shift_right_logical(column, 4)
    table = jnp.where(field == 0, peak, jnp.where(field == 1, total, jnp.where(field == 2, moment, chosen)))
    lane = lax.broadcasted_iota(jnp.int32, (HEAD, LANES), 1) & (FIELD - 1)
    sub = lax.broadcasted_iota(jnp.int32, (HEAD, LANES), 0)
    tail_mask = lane == HEAD + (sub & (TAIL - 1))
    for b in range(n):
        at = (b // half) * half * CAP
        k = b % half
        head = jnp.where(lane == sub, table[at + k * HEAD:at + (k + 1) * HEAD], 0.0)
        first = at + half * HEAD + k * TAIL
        tile, place = first // HEAD * HEAD, first % HEAD
        inside = tail_mask & (sub >= place) & (sub < place + TAIL)
        line = head + jnp.where(inside, table[tile:tile + HEAD], 0.0)
        out_ref[pl.ds(me ^ owners[b], 1), :] = jnp.sum(line, axis=0, keepdims=True)


def row_stats(owners, near, far, weights):
    n = len(owners)
    vocab_dev = sum(weight.shape[1] for weight in weights)
    return pl.pallas_call(
        functools.partial(stats_kernel, owners),
        out_shape=pltpu.VMEM((n, LANES), jnp.float32),
        in_specs=[VMEM] * (2 + len(weights)),
        out_specs=VMEM,
        scratch_shapes=[pltpu.VMEM((n * CAP, vocab_dev), jnp.float32)],
        compiler_params=pltpu.CompilerParams(vmem_limit_bytes=16 * MIB),
        name="row_stats",
    )(near, far, *weights)


def scored_kernel(counts_ref, scored_ref):
    scored_ref[...] = (lax.broadcasted_iota(jnp.int32, scored_ref.shape, 1) < counts_ref[0]).astype(jnp.float32)


def scored_lanes(counts):
    return pl.pallas_call(scored_kernel, out_shape=pltpu.VMEM((HEAD, LANES), jnp.float32), in_specs=[pl.BlockSpec(memory_space=pltpu.SMEM)], out_specs=VMEM, compiler_params=pltpu.CompilerParams(vmem_limit_bytes=MIB), name='scored')(counts)


def finish_kernel(lines_ref, scored_ref, logprob_ref, entropy_ref):
    slots = logprob_ref.shape[0]
    lines = lines_ref[...]
    peak = jnp.max(lines, axis=0, keepdims=True)
    factor = jnp.exp(lines - peak)

    def field(k):
        return pltpu.roll(lines, LANES - FIELD * k, 1)

    total = jnp.sum(field(1) * factor, axis=0, keepdims=True)
    moment = jnp.sum(field(2) * factor, axis=0, keepdims=True)
    chosen = jnp.sum(field(3), axis=0, keepdims=True)
    log_total = jnp.log(total)
    scored = scored_ref[0:1] > 0.0
    logprob = jnp.where(scored, chosen - peak - log_total, 0.0)
    entropy = jnp.where(scored, peak + log_total - moment / total, 0.0)
    logprob_ref[...] = logprob[0, :slots]
    entropy_ref[...] = entropy[0, :slots]


def finish(lines, counts, slots):
    return pl.pallas_call(
        finish_kernel,
        out_shape=(jax.ShapeDtypeStruct((slots,), jnp.float32),) * 2,
        in_specs=[VMEM] * 2,
        out_specs=[VMEM] * 2,
        compiler_params=pltpu.CompilerParams(vmem_limit_bytes=4 * MIB),
        name="finish",
    )(lines, counts)


def on_device(n, hidden, norm_gain, head_weight, targets, counts):
    slots, width = hidden.shape
    block = front(hidden, norm_gain, targets)
    fetched = {}

    def with_fetch(place, after, value):
        if place not in FETCH:
            return value
        first, last = FETCH[place]
        fetched[place], value = lax.optimization_barrier((fetch(after, head_weight, first, last), value))
        return value

    block = with_fetch("first", block, block)
    blocks, owners = [block], [0]
    *steps, last = gather_masks(n)
    for i, masks in enumerate(steps):
        got = [swap(b, mask, n) for mask in masks for b in blocks]
        if i == 0:
            for k in range(len(got)):
                got[k] = with_fetch(f"got{k}", got[k - 1] if k else block, got[k])
        owners = owners + [o ^ mask for mask in masks for o in owners]
        blocks = blocks + got
    blocks = list(with_fetch("all", blocks[len(blocks) // 2 - 1], tuple(blocks)))
    near = unpack(blocks, width)
    far = with_fetch("core", near, swap(near, last[0], n))
    owners = owners + [o ^ last[0] for o in owners]
    far, counts = lax.optimization_barrier((far, scored_lanes(counts)))
    weights = [fetched[place] for place in sorted(fetched, key=lambda place: FETCH[place])]
    lines = row_stats(tuple(owners), near, far, weights)
    lines = lax.all_to_all(lines, "vocab", 0, 0, tiled=True)
    return finish(lines, counts, slots)


def solution(mesh):
    n = mesh.shape["vocab"]
    in_specs = (
        P(("req", "vocab"), None),
        P(),
        P(None, "vocab"),
        P(("req", "vocab")),
        P(("req", "vocab")),
    )
    out_specs = (P(("req", "vocab")), P(("req", "vocab")))

    def step(*args):
        return on_device(n, *args)

    return jax.shard_map(step, mesh=mesh, in_specs=in_specs, out_specs=out_specs, check_vma=False)
```

```python
import functools

import jax
import jax.numpy as jnp
from jax import lax
from jax.experimental import pallas as pl
from jax.experimental.pallas import tpu as pltpu
from jax.sharding import PartitionSpec as P

logit_scale = 256.0 / 2304.0
CAP = 10
HEAD = 8
TAIL = CAP - HEAD
LANES = 128
PER_TILE = HEAD // TAIL
FIELD = 16
VMEM = pl.BlockSpec(memory_space=pltpu.VMEM)
ANY = pl.BlockSpec(memory_space=pl.ANY)
MIB = 1024 * 1024
N_COLS = 256
FETCH = {"all": (0, 1024)}


def moves(n):
    quarter = n // 4
    if n == 16:
        return [(2 * quarter, 0), (quarter, 1), (3 * quarter, 1)], [3, 1]
    return [(k * quarter, 0) for k in (2, 1, 3)], [quarter >> k for k in range(1, quarter.bit_length())]


def move(block, shift, mask, n):
    return lax.ppermute(block, "vocab", [(i, (i + shift) % n ^ mask) for i in range(n)])


def in_hbm(array):
    return pltpu.with_memory_space_constraint(array, pltpu.HBM)


def strip_at(chunks, c):
    tile, place = divmod(c, PER_TILE)
    return slice(TAIL * place, TAIL * place + TAIL), slice((chunks + tile) * LANES, (chunks + tile + 1) * LANES)


def front_kernel(
    hidden_hbm, gain_hbm, targets_hbm, block_ref, hidden_ref, gain_ref, targets_ref, sems
):
    copies = [
        pltpu.make_async_copy(source, target, sems.at[i])
        for i, (source, target) in enumerate(
            [(hidden_hbm, hidden_ref), (gain_hbm, gain_ref), (targets_hbm, targets_ref)]
        )
    ]
    for copy in copies:
        copy.start()
    for copy in copies:
        copy.wait()
    slots, width = hidden_ref.shape
    chunks = width // LANES + 1
    values = hidden_ref[...].astype(jnp.float32)
    square_mean = jnp.sum(values * values, axis=1, keepdims=True) * (1.0 / width)
    gain = gain_ref[...].reshape(1, width)
    normed = (values * lax.rsqrt(square_mean + 1e-05) * gain).astype(jnp.bfloat16)
    lane = lax.broadcasted_iota(jnp.int32, (slots, LANES), 1)
    sub = lax.broadcasted_iota(jnp.int32, (slots, LANES), 0)
    ids = jnp.broadcast_to(targets_ref[...].reshape(1, slots), (slots, slots))
    own = lax.broadcasted_iota(jnp.int32, (slots, slots), 0) == lax.broadcasted_iota(jnp.int32, (slots, slots), 1)
    ids = jnp.sum(jnp.where(own, ids, 0).astype(jnp.float32), axis=1, keepdims=True).astype(jnp.int32)
    ids = jnp.where(lane == 0, lax.shift_right_logical(ids, 8), jnp.where(lane == 1, ids & 255, 0))
    ids = ids.astype(jnp.float32).astype(jnp.bfloat16)
    block_ref[:, :width] = normed[:HEAD]
    block_ref[:, width:width + LANES] = ids[:HEAD]
    for c in range(chunks):
        rows, columns = strip_at(chunks, c)
        chunk = ids if c == chunks - 1 else normed[:, c * LANES:(c + 1) * LANES]
        block_ref[rows, columns] = chunk[HEAD:CAP]


def front(hidden, gain, targets):
    slots, width = hidden.shape
    chunks = width // LANES + 1
    tiles = chunks + -(-chunks // PER_TILE)
    return pl.pallas_call(
        front_kernel,
        out_shape=pltpu.VMEM((HEAD, tiles * LANES), jnp.bfloat16),
        in_specs=[ANY] * 3,
        out_specs=VMEM,
        scratch_shapes=[
            pltpu.VMEM(hidden.shape, hidden.dtype),
            pltpu.VMEM(gain.shape, gain.dtype),
            pltpu.VMEM(targets.shape, targets.dtype),
            pltpu.SemaphoreType.DMA((3,)),
        ],
        compiler_params=pltpu.CompilerParams(vmem_limit_bytes=4 * MIB),
        name="norm_and_pack",
    )(in_hbm(hidden), in_hbm(gain), in_hbm(targets))


def fetch_kernel(first, after_ref, weight_ref, out_ref, sem):
    del after_ref
    copy = pltpu.make_async_copy(weight_ref.at[:, pl.ds(first, out_ref.shape[1])], out_ref, sem)
    copy.start()
    copy.wait()


def fetch(after, weight, first, last):
    shape = (weight.shape[0], last - first)
    return pl.pallas_call(
        functools.partial(fetch_kernel, first),
        out_shape=pltpu.VMEM(shape, weight.dtype),
        in_specs=[ANY] * 2,
        out_specs=VMEM,
        scratch_shapes=[pltpu.SemaphoreType.DMA],
        cost_estimate=pl.CostEstimate(flops=0, bytes_accessed=2 * shape[0] * shape[1], transcendentals=0),
        compiler_params=pltpu.CompilerParams(vmem_limit_bytes=MIB),
        name="fetch_weights",
    )(after, in_hbm(weight))


def unpack_kernel(*refs):
    *blocks, out_ref = refs
    base = len(blocks) * HEAD
    chunks = out_ref.shape[1] // LANES
    for b, ref in enumerate(blocks):
        out_ref[b * HEAD:(b + 1) * HEAD, :] = ref[:, :chunks * LANES]
        for c in range(chunks):
            rows, columns = strip_at(chunks, c)
            out_ref[base + TAIL * b:base + TAIL * (b + 1), c * LANES:(c + 1) * LANES] = ref[rows, columns]


def unpack(blocks, width):
    return pl.pallas_call(
        unpack_kernel,
        out_shape=pltpu.VMEM((len(blocks) * CAP, width + LANES), jnp.bfloat16),
        in_specs=[VMEM] * len(blocks),
        out_specs=VMEM,
        compiler_params=pltpu.CompilerParams(vmem_limit_bytes=4 * MIB),
        name="unpack",
    )(*blocks)


def stats_kernel(owners, near_ref, far_ref, *refs):
    *weight_refs, out_ref, logits_ref = refs
    n = len(owners)
    half = n // 2
    width = near_ref.shape[1] - LANES
    vocab_dev = logits_ref.shape[1]
    m = n * CAP
    me = lax.axis_index("vocab")
    rows = jnp.concatenate([near_ref[:, :width], far_ref[:, :width]], axis=0)
    ids = jnp.concatenate([near_ref[:, width:], far_ref[:, width:]], axis=0).astype(jnp.float32)
    wanted = (ids[:, 0:1] * 256.0 + ids[:, 1:2]).astype(jnp.int32) - me * vocab_dev
    peak, first = None, 0
    for ref in weight_refs:
        for j in range(0, ref.shape[1], N_COLS):
            z = jnp.dot(rows, ref[:, j:j + N_COLS], preferred_element_type=jnp.float32) * logit_scale
            logits_ref[:, first:first + N_COLS] = z
            first += N_COLS
            for k in range(0, N_COLS, LANES):
                part = z[:, k:k + LANES]
                peak = part if peak is None else jnp.maximum(peak, part)
    peak = jnp.max(peak, axis=1, keepdims=True)
    total = jnp.zeros((m, LANES), jnp.float32)
    moment = jnp.zeros((m, LANES), jnp.float32)
    chosen = jnp.zeros((m, LANES), jnp.float32)
    column = lax.broadcasted_iota(jnp.int32, (m, LANES), 1)
    for j in range(0, vocab_dev, LANES):
        z = logits_ref[:, j:j + LANES]
        e = jnp.exp(z - peak)
        total += e
        moment += e * z
        chosen += jnp.where(column == wanted - j, z, 0.0)
    total = jnp.sum(total, axis=1, keepdims=True)
    moment = jnp.sum(moment, axis=1, keepdims=True)
    chosen = jnp.sum(chosen, axis=1, keepdims=True)
    field = lax.shift_right_logical(column, 4)
    table = jnp.where(field == 0, peak, jnp.where(field == 1, total, jnp.where(field == 2, moment, chosen)))
    lane = lax.broadcasted_iota(jnp.int32, (HEAD, LANES), 1) & (FIELD - 1)
    sub = lax.broadcasted_iota(jnp.int32, (HEAD, LANES), 0)
    tail_mask = lane == HEAD + (sub & (TAIL - 1))
    for b in range(n):
        at = (b // half) * half * CAP
        k = b % half
        head = jnp.where(lane == sub, table[at + k * HEAD:at + (k + 1) * HEAD], 0.0)
        first = at + half * HEAD + k * TAIL
        tile, place = first // HEAD * HEAD, first % HEAD
        inside = tail_mask & (sub >= place) & (sub < place + TAIL)
        line = head + jnp.where(inside, table[tile:tile + HEAD], 0.0)
        shift, mask = owners[b]
        to = lax.rem(me + n - shift, n) ^ mask
        out_ref[pl.ds(to, 1), :] = jnp.sum(line, axis=0, keepdims=True)


def row_stats(owners, near, far, weights):
    n = len(owners)
    vocab_dev = sum(weight.shape[1] for weight in weights)
    return pl.pallas_call(
        functools.partial(stats_kernel, owners),
        out_shape=pltpu.VMEM((n, LANES), jnp.float32),
        in_specs=[VMEM] * (2 + len(weights)),
        out_specs=VMEM,
        scratch_shapes=[pltpu.VMEM((n * CAP, vocab_dev), jnp.float32)],
        compiler_params=pltpu.CompilerParams(vmem_limit_bytes=16 * MIB),
        name="row_stats",
    )(near, far, *weights)


def scored_kernel(counts_ref, scored_ref):
    scored_ref[...] = (lax.broadcasted_iota(jnp.int32, scored_ref.shape, 1) < counts_ref[0]).astype(jnp.float32)


def scored_lanes(counts):
    return pl.pallas_call(scored_kernel, out_shape=pltpu.VMEM((HEAD, LANES), jnp.float32), in_specs=[pl.BlockSpec(memory_space=pltpu.SMEM)], out_specs=VMEM, compiler_params=pltpu.CompilerParams(vmem_limit_bytes=MIB), name='scored')(counts)


def finish_kernel(lines_ref, scored_ref, logprob_ref, entropy_ref):
    slots = logprob_ref.shape[0]
    lines = lines_ref[...]
    peak = jnp.max(lines, axis=0, keepdims=True)
    factor = jnp.exp(lines - peak)

    def field(k):
        return pltpu.roll(lines, LANES - FIELD * k, 1)

    total = jnp.sum(field(1) * factor, axis=0, keepdims=True)
    moment = jnp.sum(field(2) * factor, axis=0, keepdims=True)
    chosen = jnp.sum(field(3), axis=0, keepdims=True)
    log_total = jnp.log(total)
    scored = scored_ref[0:1] > 0.0
    logprob = jnp.where(scored, chosen - peak - log_total, 0.0)
    entropy = jnp.where(scored, peak + log_total - moment / total, 0.0)
    logprob_ref[...] = logprob[0, :slots]
    entropy_ref[...] = entropy[0, :slots]


def finish(lines, scored, slots):
    return pl.pallas_call(
        finish_kernel,
        out_shape=(jax.ShapeDtypeStruct((slots,), jnp.float32),) * 2,
        in_specs=[VMEM] * 2,
        out_specs=[VMEM] * 2,
        compiler_params=pltpu.CompilerParams(vmem_limit_bytes=4 * MIB),
        name="finish",
    )(lines, scored)


def on_device(n, hidden, norm_gain, head_weight, targets, counts):
    slots, width = hidden.shape
    block = front(hidden, norm_gain, targets)
    fetched = {}

    def with_fetch(place, after, value):
        if place not in FETCH:
            return value
        first, last = FETCH[place]
        fetched[place], value = lax.optimization_barrier((fetch(after, head_weight, first, last), value))
        return value

    shifts, masks = moves(n)
    blocks = [block] + [move(block, shift, mask, n) for shift, mask in shifts]
    owners = [(0, 0)] + shifts
    for mask in masks[:-1]:
        blocks = blocks + [move(b, 0, mask, n) for b in blocks]
        owners = owners + [(s, m ^ mask) for s, m in owners]
    blocks = list(with_fetch("all", blocks[len(blocks) // 2 - 1], tuple(blocks)))
    near = unpack(blocks, width)
    far = with_fetch("core", near, move(near, 0, masks[-1], n))
    far, scored = lax.optimization_barrier((far, scored_lanes(counts)))
    owners = owners + [(s, m ^ masks[-1]) for s, m in owners]
    weights = [fetched[place] for place in sorted(fetched, key=lambda place: FETCH[place])]
    lines = row_stats(tuple(owners), near, far, weights)
    lines = lax.all_to_all(lines, "vocab", 0, 0, tiled=True)
    return finish(lines, scored, slots)


def solution(mesh):
    n = mesh.shape["vocab"]
    in_specs = (
        P(("req", "vocab"), None),
        P(),
        P(None, "vocab"),
        P(("req", "vocab")),
        P(("req", "vocab")),
    )
    out_specs = (P(("req", "vocab")), P(("req", "vocab")))

    def step(*args):
        return on_device(n, *args)

    return jax.shard_map(step, mesh=mesh, in_specs=in_specs, out_specs=out_specs, check_vma=False)
```

```python
import functools

import jax
import jax.numpy as jnp
from jax import lax
from jax.experimental import pallas as pl
from jax.experimental.pallas import tpu as pltpu
from jax.sharding import PartitionSpec as P

logit_scale = 256.0 / 2304.0
CAP = 10
HEAD = 8
TAIL = CAP - HEAD
LANES = 128
PER_TILE = HEAD // TAIL
FIELD = 16
VMEM = pl.BlockSpec(memory_space=pltpu.VMEM)
ANY = pl.BlockSpec(memory_space=pl.ANY)
MIB = 1024 * 1024
N_COLS = 256
ROWS_STEP = 128


def moves(n):
    quarter = n // 4
    if n == 16:
        return [(quarter, 1), (2 * quarter, 0), (3 * quarter, 1)], [3, 1]
    return [(k * quarter, 0) for k in (1, 2, 3)], [quarter >> k for k in range(1, quarter.bit_length())]


def move(block, shift, mask, n):
    return lax.ppermute(block, "vocab", [(i, (i + shift) % n ^ mask) for i in range(n)])


def in_hbm(array):
    return pltpu.with_memory_space_constraint(array, pltpu.HBM)


def strip_at(chunks, c):
    tile, place = divmod(c, PER_TILE)
    return slice(TAIL * place, TAIL * place + TAIL), slice((chunks + tile) * LANES, (chunks + tile + 1) * LANES)


def front_kernel(
    hidden_hbm, gain_hbm, targets_hbm, block_ref, hidden_ref, gain_ref, targets_ref, sems
):
    copies = [
        pltpu.make_async_copy(source, target, sems.at[i])
        for i, (source, target) in enumerate(
            [(hidden_hbm, hidden_ref), (gain_hbm, gain_ref), (targets_hbm, targets_ref)]
        )
    ]
    for copy in copies:
        copy.start()
    for copy in copies:
        copy.wait()
    slots, width = hidden_ref.shape
    chunks = width // LANES + 1
    values = hidden_ref[...].astype(jnp.float32)
    square_mean = jnp.sum(values * values, axis=1, keepdims=True) * (1.0 / width)
    gain = gain_ref[...].reshape(1, width)
    normed = (values * lax.rsqrt(square_mean + 1e-05) * gain).astype(jnp.bfloat16)
    lane = lax.broadcasted_iota(jnp.int32, (slots, LANES), 1)
    sub = lax.broadcasted_iota(jnp.int32, (slots, LANES), 0)
    ids = jnp.broadcast_to(targets_ref[...].reshape(1, slots), (slots, slots))
    own = lax.broadcasted_iota(jnp.int32, (slots, slots), 0) == lax.broadcasted_iota(jnp.int32, (slots, slots), 1)
    ids = jnp.sum(jnp.where(own, ids, 0).astype(jnp.float32), axis=1, keepdims=True).astype(jnp.int32)
    ids = jnp.where(lane == 0, lax.shift_right_logical(ids, 8), jnp.where(lane == 1, ids & 255, 0))
    ids = ids.astype(jnp.float32).astype(jnp.bfloat16)
    block_ref[:, :width] = normed[:HEAD]
    block_ref[:, width:width + LANES] = ids[:HEAD]
    for c in range(chunks):
        rows, columns = strip_at(chunks, c)
        chunk = ids if c == chunks - 1 else normed[:, c * LANES:(c + 1) * LANES]
        block_ref[rows, columns] = chunk[HEAD:CAP]


def front(hidden, gain, targets):
    slots, width = hidden.shape
    chunks = width // LANES + 1
    tiles = chunks + -(-chunks // PER_TILE)
    return pl.pallas_call(
        front_kernel,
        out_shape=pltpu.VMEM((HEAD, tiles * LANES), jnp.bfloat16),
        in_specs=[ANY] * 3,
        out_specs=VMEM,
        scratch_shapes=[
            pltpu.VMEM(hidden.shape, hidden.dtype),
            pltpu.VMEM(gain.shape, gain.dtype),
            pltpu.VMEM(targets.shape, targets.dtype),
            pltpu.SemaphoreType.DMA((3,)),
        ],
        compiler_params=pltpu.CompilerParams(vmem_limit_bytes=4 * MIB),
        name="norm_and_pack",
    )(in_hbm(hidden), in_hbm(gain), in_hbm(targets))


def fetch_kernel(after_ref, weight_ref, out_ref, sem):
    del after_ref
    copy = pltpu.make_async_copy(weight_ref, out_ref, sem)
    copy.start()
    copy.wait()


def fetch(after, weight):
    return pl.pallas_call(
        fetch_kernel,
        out_shape=pltpu.VMEM(weight.shape, weight.dtype),
        in_specs=[ANY] * 2,
        out_specs=VMEM,
        scratch_shapes=[pltpu.SemaphoreType.DMA],
        cost_estimate=pl.CostEstimate(flops=0, bytes_accessed=2 * weight.size, transcendentals=0),
        compiler_params=pltpu.CompilerParams(vmem_limit_bytes=MIB),
        name="fetch_weights",
    )(after, in_hbm(weight))


def unpack_kernel(*refs):
    *blocks, out_ref = refs
    base = len(blocks) * HEAD
    chunks = out_ref.shape[1] // LANES
    for b, ref in enumerate(blocks):
        out_ref[b * HEAD:(b + 1) * HEAD, :] = ref[:, :chunks * LANES]
        for c in range(chunks):
            rows, columns = strip_at(chunks, c)
            out_ref[base + TAIL * b:base + TAIL * (b + 1), c * LANES:(c + 1) * LANES] = ref[rows, columns]


def unpack(blocks, width):
    return pl.pallas_call(
        unpack_kernel,
        out_shape=pltpu.VMEM((len(blocks) * CAP, width + LANES), jnp.bfloat16),
        in_specs=[VMEM] * len(blocks),
        out_specs=VMEM,
        compiler_params=pltpu.CompilerParams(vmem_limit_bytes=4 * MIB),
        name="unpack",
    )(*blocks)


def stats_kernel(n, owners, rows_in, weight_ref, out_ref, logits_ref):
    count = len(owners)
    width = rows_in.shape[1] - LANES
    vocab_dev = logits_ref.shape[1]
    used, m = rows_in.shape[0], logits_ref.shape[0]
    me = lax.axis_index("vocab")
    rows, ids = rows_in[:, :width], rows_in[:, width:]
    if m > used:
        rows = jnp.concatenate([rows, jnp.zeros((m - used, width), rows.dtype)], axis=0)
        ids = jnp.concatenate([ids, jnp.zeros((m - used, LANES), ids.dtype)], axis=0)
    ids = ids.astype(jnp.float32)
    wanted = (ids[:, 0:1] * 256.0 + ids[:, 1:2]).astype(jnp.int32) - me * vocab_dev
    peak = None
    for j in range(0, vocab_dev, N_COLS):
        z = jnp.dot(rows, weight_ref[:, j:j + N_COLS], preferred_element_type=jnp.float32) * logit_scale
        logits_ref[:, j:j + N_COLS] = z
        for k in range(0, N_COLS, LANES):
            part = z[:, k:k + LANES]
            peak = part if peak is None else jnp.maximum(peak, part)
    m = used
    peak = jnp.max(peak[:m], axis=1, keepdims=True)
    wanted = wanted[:m]
    total = jnp.zeros((m, LANES), jnp.float32)
    moment = jnp.zeros((m, LANES), jnp.float32)
    chosen = jnp.zeros((m, LANES), jnp.float32)
    column = lax.broadcasted_iota(jnp.int32, (m, LANES), 1)
    for j in range(0, vocab_dev, LANES):
        z = logits_ref[:m, j:j + LANES]
        e = jnp.exp(z - peak)
        total += e
        moment += e * z
        chosen += jnp.where(column == wanted - j, z, 0.0)
    total = jnp.sum(total, axis=1, keepdims=True)
    moment = jnp.sum(moment, axis=1, keepdims=True)
    chosen = jnp.sum(chosen, axis=1, keepdims=True)
    field = lax.shift_right_logical(column, 4)
    table = jnp.where(field == 0, peak, jnp.where(field == 1, total, jnp.where(field == 2, moment, chosen)))
    lane = lax.broadcasted_iota(jnp.int32, (HEAD, LANES), 1) & (FIELD - 1)
    sub = lax.broadcasted_iota(jnp.int32, (HEAD, LANES), 0)
    tail_mask = lane == HEAD + (sub & (TAIL - 1))
    for b in range(count):
        head = jnp.where(lane == sub, table[b * HEAD:(b + 1) * HEAD], 0.0)
        at = count * HEAD + b * TAIL
        tile, place = at // HEAD * HEAD, at % HEAD
        inside = tail_mask & (sub >= place) & (sub < place + TAIL)
        line = head + jnp.where(inside, table[tile:tile + HEAD], 0.0)
        shift, mask = owners[b]
        to = lax.rem(me + n - shift, n) ^ mask
        out_ref[pl.ds(to, 1), :] = jnp.sum(line, axis=0, keepdims=True)


def more_stats_kernel(n, owners, rows_in, weight_ref, lines_in, out_ref, logits_ref):
    del lines_in
    stats_kernel(n, owners, rows_in, weight_ref, out_ref, logits_ref)


def row_stats(n, owners, rows, weight, lines=None):
    vocab_dev = weight.shape[1]
    more = lines is not None
    return pl.pallas_call(
        functools.partial(more_stats_kernel if more else stats_kernel, n, owners),
        out_shape=pltpu.VMEM((n, LANES), jnp.float32),
        in_specs=[VMEM] * 2 + [ANY] * more,
        out_specs=VMEM,
        input_output_aliases={2: 0} if more else {},
        scratch_shapes=[pltpu.VMEM((-(-rows.shape[0] // ROWS_STEP) * ROWS_STEP, vocab_dev), jnp.float32)],
        cost_estimate=pl.CostEstimate(flops=2 * rows.size * vocab_dev, bytes_accessed=0, transcendentals=0),
        compiler_params=pltpu.CompilerParams(vmem_limit_bytes=16 * MIB),
        name="row_stats",
    )(rows, weight, *([lines] if more else []))


def scored_kernel(counts_ref, scored_ref):
    scored_ref[...] = (lax.broadcasted_iota(jnp.int32, scored_ref.shape, 1) < counts_ref[0]).astype(jnp.float32)


def scored_lanes(counts):
    return pl.pallas_call(
        scored_kernel,
        out_shape=pltpu.VMEM((HEAD, LANES), jnp.float32),
        in_specs=[pl.BlockSpec(memory_space=pltpu.SMEM)],
        out_specs=VMEM,
        compiler_params=pltpu.CompilerParams(vmem_limit_bytes=MIB),
        name="scored",
    )(counts)


def finish_kernel(lines_ref, scored_ref, logprob_ref, entropy_ref):
    slots = logprob_ref.shape[0]
    lines = lines_ref[...]
    peak = jnp.max(lines, axis=0, keepdims=True)
    factor = jnp.exp(lines - peak)

    def field(k):
        return pltpu.roll(lines, LANES - FIELD * k, 1)

    total = jnp.sum(field(1) * factor, axis=0, keepdims=True)
    moment = jnp.sum(field(2) * factor, axis=0, keepdims=True)
    chosen = jnp.sum(field(3), axis=0, keepdims=True)
    log_total = jnp.log(total)
    scored = scored_ref[0:1] > 0.0
    logprob = jnp.where(scored, chosen - peak - log_total, 0.0)
    entropy = jnp.where(scored, peak + log_total - moment / total, 0.0)
    logprob_ref[...] = logprob[0, :slots]
    entropy_ref[...] = entropy[0, :slots]


def finish(lines, scored, slots):
    return pl.pallas_call(
        finish_kernel,
        out_shape=(jax.ShapeDtypeStruct((slots,), jnp.float32),) * 2,
        in_specs=[VMEM] * 2,
        out_specs=[VMEM] * 2,
        compiler_params=pltpu.CompilerParams(vmem_limit_bytes=4 * MIB),
        name="finish",
    )(lines, scored)


def on_device(n, hidden, norm_gain, head_weight, targets, counts):
    slots, width = hidden.shape
    block = front(hidden, norm_gain, targets)
    shifts, masks = moves(n)
    blocks = [block] + [move(block, shift, mask, n) for shift, mask in shifts]
    owners = [(0, 0)] + shifts
    for mask in masks[:-1]:
        blocks = blocks + [move(b, 0, mask, n) for b in blocks]
        owners = owners + [(s, m ^ mask) for s, m in owners]
    beside = fetch(blocks[len(blocks) // 2 - 1], head_weight), scored_lanes(counts)
    weight, scored, *blocks = lax.optimization_barrier((*beside, *blocks))
    near = unpack(blocks, width)
    far = move(near, 0, masks[-1], n)
    lines = row_stats(n, tuple(owners), near, weight)
    owners = [(s, m ^ masks[-1]) for s, m in owners]
    lines = row_stats(n, tuple(owners), far, weight, lines)
    lines = lax.all_to_all(lines, "vocab", 0, 0, tiled=True)
    return finish(lines, scored, slots)


def solution(mesh):
    n = mesh.shape["vocab"]
    in_specs = (
        P(("req", "vocab"), None),
        P(),
        P(None, "vocab"),
        P(("req", "vocab")),
        P(("req", "vocab")),
    )
    out_specs = (P(("req", "vocab")), P(("req", "vocab")))

    def step(*args):
        return on_device(n, *args)

    return jax.shard_map(step, mesh=mesh, in_specs=in_specs, out_specs=out_specs, check_vma=False)
```

```python
import functools

import jax
import jax.numpy as jnp
from jax import lax
from jax.experimental import pallas as pl
from jax.experimental.pallas import tpu as pltpu
from jax.sharding import PartitionSpec as P

logit_scale = 256.0 / 2304.0
CAP = 10
HEAD = 8
TAIL = CAP - HEAD
LANES = 128
PER_TILE = HEAD // TAIL
FIELD = 16
VMEM = pl.BlockSpec(memory_space=pltpu.VMEM)
ANY = pl.BlockSpec(memory_space=pl.ANY)
MIB = 1024 * 1024
N_COLS = 256
ROWS_STEP = 128


def moves(n):
    quarter = n // 4
    if n == 16:
        return [(quarter, 1), (2 * quarter, 0), (3 * quarter, 1), (3 * quarter, 2)], [3, 1]
    return [(k * quarter, 0) for k in (1, 2, 3)], [quarter >> k for k in range(1, quarter.bit_length())]


def move(block, shift, mask, n):
    return lax.ppermute(block, "vocab", [(i, (i + shift) % n ^ mask) for i in range(n)])


def in_hbm(array):
    return pltpu.with_memory_space_constraint(array, pltpu.HBM)


def strip_at(chunks, c):
    tile, place = divmod(c, PER_TILE)
    return slice(TAIL * place, TAIL * place + TAIL), slice((chunks + tile) * LANES, (chunks + tile + 1) * LANES)


def front_kernel(
    hidden_hbm, gain_hbm, targets_hbm, block_ref, hidden_ref, gain_ref, targets_ref, sems
):
    cut = hidden_hbm.shape[1] // LANES // 2 * LANES
    pairs = [(hidden_hbm.at[:, :cut], hidden_ref.at[:, :cut]), (hidden_hbm.at[:, cut:], hidden_ref.at[:, cut:])]
    pairs += [(gain_hbm, gain_ref), (targets_hbm, targets_ref)]
    copies = [pltpu.make_async_copy(source, target, sems.at[i]) for i, (source, target) in enumerate(pairs)]
    for copy in copies:
        copy.start()
    for copy in copies:
        copy.wait()
    slots, width = hidden_ref.shape
    chunks = width // LANES + 1
    values = hidden_ref[...].astype(jnp.float32)
    square_mean = jnp.sum(values * values, axis=1, keepdims=True) * (1.0 / width)
    gain = gain_ref[...].reshape(1, width)
    normed = (values * lax.rsqrt(square_mean + 1e-05) * gain).astype(jnp.bfloat16)
    lane = lax.broadcasted_iota(jnp.int32, (slots, LANES), 1)
    sub = lax.broadcasted_iota(jnp.int32, (slots, LANES), 0)
    ids = jnp.broadcast_to(targets_ref[...].reshape(1, slots), (slots, slots))
    own = lax.broadcasted_iota(jnp.int32, (slots, slots), 0) == lax.broadcasted_iota(jnp.int32, (slots, slots), 1)
    ids = jnp.sum(jnp.where(own, ids, 0).astype(jnp.float32), axis=1, keepdims=True).astype(jnp.int32)
    ids = jnp.where(lane == 0, lax.shift_right_logical(ids, 8), jnp.where(lane == 1, ids & 255, 0))
    ids = ids.astype(jnp.float32).astype(jnp.bfloat16)
    block_ref[:, :width] = normed[:HEAD]
    block_ref[:, width:width + LANES] = ids[:HEAD]
    for c in range(chunks):
        rows, columns = strip_at(chunks, c)
        chunk = ids if c == chunks - 1 else normed[:, c * LANES:(c + 1) * LANES]
        block_ref[rows, columns] = chunk[HEAD:CAP]


def front(hidden, gain, targets):
    slots, width = hidden.shape
    chunks = width // LANES + 1
    tiles = chunks + -(-chunks // PER_TILE)
    return pl.pallas_call(
        front_kernel,
        out_shape=pltpu.VMEM((HEAD, tiles * LANES), jnp.bfloat16),
        in_specs=[ANY] * 3,
        out_specs=VMEM,
        scratch_shapes=[
            pltpu.VMEM(hidden.shape, hidden.dtype),
            pltpu.VMEM(gain.shape, gain.dtype),
            pltpu.VMEM(targets.shape, targets.dtype),
            pltpu.SemaphoreType.DMA((4,)),
        ],
        compiler_params=pltpu.CompilerParams(vmem_limit_bytes=4 * MIB),
        name="norm_and_pack",
    )(in_hbm(hidden), in_hbm(gain), in_hbm(targets))


def fetch_kernel(after_ref, weight_ref, out_ref, sem):
    del after_ref
    copy = pltpu.make_async_copy(weight_ref, out_ref, sem)
    copy.start()
    copy.wait()


def fetch(after, weight):
    return pl.pallas_call(
        fetch_kernel,
        out_shape=pltpu.VMEM(weight.shape, weight.dtype),
        in_specs=[ANY] * 2,
        out_specs=VMEM,
        scratch_shapes=[pltpu.SemaphoreType.DMA],
        cost_estimate=pl.CostEstimate(flops=0, bytes_accessed=2 * weight.size, transcendentals=0),
        compiler_params=pltpu.CompilerParams(vmem_limit_bytes=MIB),
        name="fetch_weights",
    )(after, in_hbm(weight))


def unpack_kernel(*refs):
    *blocks, out_ref = refs
    base = len(blocks) * HEAD
    chunks = out_ref.shape[1] // LANES
    for b, ref in enumerate(blocks):
        out_ref[b * HEAD:(b + 1) * HEAD, :] = ref[:, :chunks * LANES]
        for c in range(chunks):
            rows, columns = strip_at(chunks, c)
            out_ref[base + TAIL * b:base + TAIL * (b + 1), c * LANES:(c + 1) * LANES] = ref[rows, columns]


def unpack(blocks, width):
    return pl.pallas_call(
        unpack_kernel,
        out_shape=pltpu.VMEM((len(blocks) * CAP, width + LANES), jnp.bfloat16),
        in_specs=[VMEM] * len(blocks),
        out_specs=VMEM,
        compiler_params=pltpu.CompilerParams(vmem_limit_bytes=4 * MIB),
        name="unpack",
    )(*blocks)


def stats_kernel(n, owners, rows_in, weight_ref, out_ref, logits_ref):
    count = len(owners)
    width = rows_in.shape[1] - LANES
    vocab_dev = logits_ref.shape[1]
    used, m = rows_in.shape[0], logits_ref.shape[0]
    me = lax.axis_index("vocab")
    rows, ids = rows_in[:, :width], rows_in[:, width:]
    if m > used:
        rows = jnp.concatenate([rows, jnp.zeros((m - used, width), rows.dtype)], axis=0)
        ids = jnp.concatenate([ids, jnp.zeros((m - used, LANES), ids.dtype)], axis=0)
    ids = ids.astype(jnp.float32)
    wanted = (ids[:, 0:1] * 256.0 + ids[:, 1:2]).astype(jnp.int32) - me * vocab_dev
    peak = None
    for j in range(0, vocab_dev, N_COLS):
        z = jnp.dot(rows, weight_ref[:, j:j + N_COLS], preferred_element_type=jnp.float32) * logit_scale
        logits_ref[:, j:j + N_COLS] = z
        for k in range(0, N_COLS, LANES):
            part = z[:, k:k + LANES]
            peak = part if peak is None else jnp.maximum(peak, part)
    m = used
    peak = jnp.max(peak[:m], axis=1, keepdims=True)
    wanted = wanted[:m]
    total = jnp.zeros((m, LANES), jnp.float32)
    moment = jnp.zeros((m, LANES), jnp.float32)
    chosen = jnp.zeros((m, LANES), jnp.float32)
    column = lax.broadcasted_iota(jnp.int32, (m, LANES), 1)
    for j in range(0, vocab_dev, LANES):
        z = logits_ref[:m, j:j + LANES]
        e = jnp.exp(z - peak)
        total += e
        moment += e * z
        chosen += jnp.where(column == wanted - j, z, 0.0)
    total = jnp.sum(total, axis=1, keepdims=True)
    moment = jnp.sum(moment, axis=1, keepdims=True)
    chosen = jnp.sum(chosen, axis=1, keepdims=True)
    field = lax.shift_right_logical(column, 4)
    table = jnp.where(field == 0, peak, jnp.where(field == 1, total, jnp.where(field == 2, moment, chosen)))
    lane = lax.broadcasted_iota(jnp.int32, (HEAD, LANES), 1) & (FIELD - 1)
    sub = lax.broadcasted_iota(jnp.int32, (HEAD, LANES), 0)
    tail_mask = lane == HEAD + (sub & (TAIL - 1))
    for b in range(count):
        head = jnp.where(lane == sub, table[b * HEAD:(b + 1) * HEAD], 0.0)
        at = count * HEAD + b * TAIL
        tile, place = at // HEAD * HEAD, at % HEAD
        inside = tail_mask & (sub >= place) & (sub < place + TAIL)
        line = head + jnp.where(inside, table[tile:tile + HEAD], 0.0)
        shift, mask = owners[b]
        to = lax.rem(me + n - shift, n) ^ mask
        out_ref[pl.ds(to, 1), :] = jnp.sum(line, axis=0, keepdims=True)


def more_stats_kernel(n, owners, rows_in, weight_ref, lines_in, out_ref, logits_ref):
    del lines_in
    stats_kernel(n, owners, rows_in, weight_ref, out_ref, logits_ref)


def row_stats(n, owners, rows, weight, lines=None):
    vocab_dev = weight.shape[1]
    more = lines is not None
    return pl.pallas_call(
        functools.partial(more_stats_kernel if more else stats_kernel, n, owners),
        out_shape=pltpu.VMEM((n, LANES), jnp.float32),
        in_specs=[VMEM] * 2 + [ANY] * more,
        out_specs=VMEM,
        input_output_aliases={2: 0} if more else {},
        scratch_shapes=[pltpu.VMEM((-(-rows.shape[0] // ROWS_STEP) * ROWS_STEP, vocab_dev), jnp.float32)],
        cost_estimate=pl.CostEstimate(flops=2 * rows.size * vocab_dev, bytes_accessed=0, transcendentals=0),
        compiler_params=pltpu.CompilerParams(vmem_limit_bytes=16 * MIB),
        name="row_stats",
    )(rows, weight, *([lines] if more else []))


def scored_kernel(counts_ref, scored_ref):
    scored_ref[...] = (lax.broadcasted_iota(jnp.int32, scored_ref.shape, 1) < counts_ref[0]).astype(jnp.float32)


def scored_lanes(counts):
    return pl.pallas_call(
        scored_kernel,
        out_shape=pltpu.VMEM((HEAD, LANES), jnp.float32),
        in_specs=[pl.BlockSpec(memory_space=pltpu.SMEM)],
        out_specs=VMEM,
        compiler_params=pltpu.CompilerParams(vmem_limit_bytes=MIB),
        name="scored",
    )(counts)


def finish_kernel(lines_ref, scored_ref, logprob_ref, entropy_ref):
    slots = logprob_ref.shape[0]
    lines = lines_ref[...]
    peak = jnp.max(lines, axis=0, keepdims=True)
    factor = jnp.exp(lines - peak)

    def field(k):
        return pltpu.roll(lines, LANES - FIELD * k, 1)

    total = jnp.sum(field(1) * factor, axis=0, keepdims=True)
    moment = jnp.sum(field(2) * factor, axis=0, keepdims=True)
    chosen = jnp.sum(field(3), axis=0, keepdims=True)
    log_total = jnp.log(total)
    scored = scored_ref[0:1] > 0.0
    logprob = jnp.where(scored, chosen - peak - log_total, 0.0)
    entropy = jnp.where(scored, peak + log_total - moment / total, 0.0)
    logprob_ref[...] = logprob[0, :slots]
    entropy_ref[...] = entropy[0, :slots]


def finish(lines, scored, slots):
    return pl.pallas_call(
        finish_kernel,
        out_shape=(jax.ShapeDtypeStruct((slots,), jnp.float32),) * 2,
        in_specs=[VMEM] * 2,
        out_specs=[VMEM] * 2,
        compiler_params=pltpu.CompilerParams(vmem_limit_bytes=4 * MIB),
        name="finish",
    )(lines, scored)


def on_device(n, hidden, norm_gain, head_weight, targets, counts):
    slots, width = hidden.shape
    block = front(hidden, norm_gain, targets)
    direct, masks = moves(n)
    have = {(0, 0): block}
    for shift, mask in direct:
        have[shift, mask] = move(block, shift, mask, n)
    for by in masks[:-1]:
        for (shift, mask), held in list(have.items()):
            if (shift, mask ^ by) not in have:
                have[shift, mask ^ by] = move(held, 0, by, n)
    beside = fetch(have[direct[1]], head_weight), scored_lanes(counts)
    weight, scored, *blocks = lax.optimization_barrier((*beside, *have.values()))
    near = unpack(blocks, width)
    far = move(near, 0, masks[-1], n)
    owners = tuple(have)
    lines = row_stats(n, owners, near, weight)
    owners = tuple((shift, mask ^ masks[-1]) for shift, mask in owners)
    lines = row_stats(n, owners, far, weight, lines)
    lines = lax.all_to_all(lines, "vocab", 0, 0, tiled=True)
    return finish(lines, scored, slots)


def solution(mesh):
    n = mesh.shape["vocab"]
    in_specs = (
        P(("req", "vocab"), None),
        P(),
        P(None, "vocab"),
        P(("req", "vocab")),
        P(("req", "vocab")),
    )
    out_specs = (P(("req", "vocab")), P(("req", "vocab")))

    def step(*args):
        return on_device(n, *args)

    return jax.shard_map(step, mesh=mesh, in_specs=in_specs, out_specs=out_specs, check_vma=False)
```

```python
import functools

import jax
import jax.numpy as jnp
from jax import lax
from jax.experimental import pallas as pl
from jax.experimental.pallas import tpu as pltpu
from jax.sharding import PartitionSpec as P

logit_scale = 256.0 / 2304.0
CAP = 10
HEAD = 8
TAIL = CAP - HEAD
LANES = 128
PER_TILE = HEAD // TAIL
FIELD = 16
VMEM = pl.BlockSpec(memory_space=pltpu.VMEM)
ANY = pl.BlockSpec(memory_space=pl.ANY)
MIB = 1024 * 1024
N_COLS = 512
ROWS_STEP = 128


def moves(n):
    quarter = n // 4
    if n == 16:
        return [(quarter, 1), (2 * quarter, 0), (3 * quarter, 1), (3 * quarter, 2)], [3, 1]
    return [(k * quarter, 0) for k in (1, 2, 3)], [quarter >> k for k in range(1, quarter.bit_length())]


def move(block, shift, mask, n):
    return lax.ppermute(block, "vocab", [(i, (i + shift) % n ^ mask) for i in range(n)])


def in_hbm(array):
    return pltpu.with_memory_space_constraint(array, pltpu.HBM)


def strip_at(chunks, c):
    tile, place = divmod(c, PER_TILE)
    return slice(TAIL * place, TAIL * place + TAIL), slice((chunks + tile) * LANES, (chunks + tile + 1) * LANES)


def front_kernel(
    hidden_hbm, gain_hbm, targets_hbm, block_ref, hidden_ref, gain_ref, targets_ref, sems
):
    cut = hidden_hbm.shape[1] // LANES // 2 * LANES
    pairs = [(hidden_hbm.at[:, :cut], hidden_ref.at[:, :cut]), (hidden_hbm.at[:, cut:], hidden_ref.at[:, cut:])]
    pairs += [(gain_hbm, gain_ref), (targets_hbm, targets_ref)]
    copies = [pltpu.make_async_copy(source, target, sems.at[i]) for i, (source, target) in enumerate(pairs)]
    for copy in copies:
        copy.start()
    for copy in copies:
        copy.wait()
    slots, width = hidden_ref.shape
    chunks = width // LANES + 1
    values = hidden_ref[...].astype(jnp.float32)
    square_mean = jnp.sum(values * values, axis=1, keepdims=True) * (1.0 / width)
    gain = gain_ref[...].reshape(1, width)
    normed = (values * lax.rsqrt(square_mean + 1e-05) * gain).astype(jnp.bfloat16)
    lane = lax.broadcasted_iota(jnp.int32, (slots, LANES), 1)
    sub = lax.broadcasted_iota(jnp.int32, (slots, LANES), 0)
    ids = jnp.broadcast_to(targets_ref[...].reshape(1, slots), (slots, slots))
    own = lax.broadcasted_iota(jnp.int32, (slots, slots), 0) == lax.broadcasted_iota(jnp.int32, (slots, slots), 1)
    ids = jnp.sum(jnp.where(own, ids, 0).astype(jnp.float32), axis=1, keepdims=True).astype(jnp.int32)
    ids = jnp.where(lane == 0, lax.shift_right_logical(ids, 8), jnp.where(lane == 1, ids & 255, 0))
    ids = ids.astype(jnp.float32).astype(jnp.bfloat16)
    block_ref[:, :width] = normed[:HEAD]
    block_ref[:, width:width + LANES] = ids[:HEAD]
    for c in range(chunks):
        rows, columns = strip_at(chunks, c)
        chunk = ids if c == chunks - 1 else normed[:, c * LANES:(c + 1) * LANES]
        block_ref[rows, columns] = chunk[HEAD:CAP]


def front(hidden, gain, targets):
    slots, width = hidden.shape
    chunks = width // LANES + 1
    tiles = chunks + -(-chunks // PER_TILE)
    return pl.pallas_call(
        front_kernel,
        out_shape=pltpu.VMEM((HEAD, tiles * LANES), jnp.bfloat16),
        in_specs=[ANY] * 3,
        out_specs=VMEM,
        scratch_shapes=[
            pltpu.VMEM(hidden.shape, hidden.dtype),
            pltpu.VMEM(gain.shape, gain.dtype),
            pltpu.VMEM(targets.shape, targets.dtype),
            pltpu.SemaphoreType.DMA((4,)),
        ],
        compiler_params=pltpu.CompilerParams(vmem_limit_bytes=4 * MIB),
        name="norm_and_pack",
    )(in_hbm(hidden), in_hbm(gain), in_hbm(targets))


def fetch_kernel(after_ref, weight_ref, out_ref, sem):
    del after_ref
    copy = pltpu.make_async_copy(weight_ref, out_ref, sem)
    copy.start()
    copy.wait()


def fetch(after, weight):
    return pl.pallas_call(
        fetch_kernel,
        out_shape=pltpu.VMEM(weight.shape, weight.dtype),
        in_specs=[ANY] * 2,
        out_specs=VMEM,
        scratch_shapes=[pltpu.SemaphoreType.DMA],
        cost_estimate=pl.CostEstimate(flops=0, bytes_accessed=2 * weight.size, transcendentals=0),
        compiler_params=pltpu.CompilerParams(vmem_limit_bytes=MIB),
        name="fetch_weights",
    )(after, in_hbm(weight))


def unpack_kernel(*refs):
    *blocks, out_ref = refs
    base = len(blocks) * HEAD
    chunks = out_ref.shape[1] // LANES
    for b, ref in enumerate(blocks):
        out_ref[b * HEAD:(b + 1) * HEAD, :] = ref[:, :chunks * LANES]
        for c in range(chunks):
            rows, columns = strip_at(chunks, c)
            out_ref[base + TAIL * b:base + TAIL * (b + 1), c * LANES:(c + 1) * LANES] = ref[rows, columns]


def unpack(blocks, width):
    return pl.pallas_call(
        unpack_kernel,
        out_shape=pltpu.VMEM((len(blocks) * CAP, width + LANES), jnp.bfloat16),
        in_specs=[VMEM] * len(blocks),
        out_specs=VMEM,
        compiler_params=pltpu.CompilerParams(vmem_limit_bytes=4 * MIB),
        name="unpack",
    )(*blocks)


def stats_kernel(n, owners, rows_in, weight_ref, out_ref, logits_ref):
    count = len(owners)
    width = rows_in.shape[1] - LANES
    vocab_dev = logits_ref.shape[1]
    used, m = rows_in.shape[0], logits_ref.shape[0]
    me = lax.axis_index("vocab")
    rows, ids = rows_in[:, :width], rows_in[:, width:]
    if m > used:
        rows = jnp.concatenate([rows, jnp.zeros((m - used, width), rows.dtype)], axis=0)
        ids = jnp.concatenate([ids, jnp.zeros((m - used, LANES), ids.dtype)], axis=0)
    ids = ids.astype(jnp.float32)
    wanted = (ids[:, 0:1] * 256.0 + ids[:, 1:2]).astype(jnp.int32) - me * vocab_dev
    peak = None
    for j in range(0, vocab_dev, N_COLS):
        z = jnp.dot(rows, weight_ref[:, j:j + N_COLS], preferred_element_type=jnp.float32) * logit_scale
        logits_ref[:, j:j + N_COLS] = z
        for k in range(0, N_COLS, LANES):
            part = z[:, k:k + LANES]
            peak = part if peak is None else jnp.maximum(peak, part)
    m = used
    peak = jnp.max(peak[:m], axis=1, keepdims=True)
    wanted = wanted[:m]
    total = jnp.zeros((m, LANES), jnp.float32)
    moment = jnp.zeros((m, LANES), jnp.float32)
    chosen = jnp.zeros((m, LANES), jnp.float32)
    column = lax.broadcasted_iota(jnp.int32, (m, LANES), 1)
    for j in range(0, vocab_dev, LANES):
        z = logits_ref[:m, j:j + LANES]
        e = jnp.exp(z - peak)
        total += e
        moment += e * z
        chosen += jnp.where(column == wanted - j, z, 0.0)
    total = jnp.sum(total, axis=1, keepdims=True)
    moment = jnp.sum(moment, axis=1, keepdims=True)
    chosen = jnp.sum(chosen, axis=1, keepdims=True)
    field = lax.shift_right_logical(column, 4)
    table = jnp.where(field == 0, peak, jnp.where(field == 1, total, jnp.where(field == 2, moment, chosen)))
    lane = lax.broadcasted_iota(jnp.int32, (HEAD, LANES), 1) & (FIELD - 1)
    sub = lax.broadcasted_iota(jnp.int32, (HEAD, LANES), 0)
    tail_mask = lane == HEAD + (sub & (TAIL - 1))
    for b in range(count):
        head = jnp.where(lane == sub, table[b * HEAD:(b + 1) * HEAD], 0.0)
        at = count * HEAD + b * TAIL
        tile, place = at // HEAD * HEAD, at % HEAD
        inside = tail_mask & (sub >= place) & (sub < place + TAIL)
        line = head + jnp.where(inside, table[tile:tile + HEAD], 0.0)
        shift, mask = owners[b]
        to = lax.rem(me + n - shift, n) ^ mask
        out_ref[pl.ds(to, 1), :] = jnp.sum(line, axis=0, keepdims=True)


def more_stats_kernel(n, owners, rows_in, weight_ref, lines_in, out_ref, logits_ref):
    del lines_in
    stats_kernel(n, owners, rows_in, weight_ref, out_ref, logits_ref)


def row_stats(n, owners, rows, weight, lines=None):
    vocab_dev = weight.shape[1]
    more = lines is not None
    return pl.pallas_call(
        functools.partial(more_stats_kernel if more else stats_kernel, n, owners),
        out_shape=pltpu.VMEM((n, LANES), jnp.float32),
        in_specs=[VMEM] * 2 + [ANY] * more,
        out_specs=VMEM,
        input_output_aliases={2: 0} if more else {},
        scratch_shapes=[pltpu.VMEM((-(-rows.shape[0] // ROWS_STEP) * ROWS_STEP, vocab_dev), jnp.float32)],
        cost_estimate=pl.CostEstimate(flops=2 * rows.size * vocab_dev, bytes_accessed=0, transcendentals=0),
        compiler_params=pltpu.CompilerParams(vmem_limit_bytes=16 * MIB),
        name="row_stats",
    )(rows, weight, *([lines] if more else []))


def scored_kernel(counts_ref, scored_ref):
    scored_ref[...] = (lax.broadcasted_iota(jnp.int32, scored_ref.shape, 1) < counts_ref[0]).astype(jnp.float32)


def scored_lanes(counts):
    return pl.pallas_call(
        scored_kernel,
        out_shape=pltpu.VMEM((HEAD, LANES), jnp.float32),
        in_specs=[pl.BlockSpec(memory_space=pltpu.SMEM)],
        out_specs=VMEM,
        compiler_params=pltpu.CompilerParams(vmem_limit_bytes=MIB),
        name="scored",
    )(counts)


def finish_kernel(lines_ref, scored_ref, logprob_hbm, entropy_hbm, logprob_ref, entropy_ref, sems):
    slots = logprob_ref.shape[0]
    lines = lines_ref[...]
    peak = jnp.max(lines, axis=0, keepdims=True)
    factor = jnp.exp(lines - peak)

    def field(k):
        return pltpu.roll(lines, LANES - FIELD * k, 1)

    total = jnp.sum(field(1) * factor, axis=0, keepdims=True)
    moment = jnp.sum(field(2) * factor, axis=0, keepdims=True)
    chosen = jnp.sum(field(3), axis=0, keepdims=True)
    log_total = jnp.log(total)
    scored = scored_ref[0:1] > 0.0
    logprob = jnp.where(scored, chosen - peak - log_total, 0.0)
    logprob_ref[...] = logprob[0, :slots]
    logprob_out = pltpu.make_async_copy(logprob_ref, logprob_hbm, sems.at[0])
    logprob_out.start()
    entropy = jnp.where(scored, peak + log_total - moment / total, 0.0)
    entropy_ref[...] = entropy[0, :slots]
    entropy_out = pltpu.make_async_copy(entropy_ref, entropy_hbm, sems.at[1])
    entropy_out.start()
    logprob_out.wait()
    entropy_out.wait()


def finish(lines, scored, slots):
    return pl.pallas_call(
        finish_kernel,
        out_shape=(jax.ShapeDtypeStruct((slots,), jnp.float32),) * 2,
        in_specs=[VMEM] * 2,
        out_specs=[pl.BlockSpec(memory_space=pltpu.HBM)] * 2,
        scratch_shapes=[pltpu.VMEM((slots,), jnp.float32)] * 2 + [pltpu.SemaphoreType.DMA((2,))],
        compiler_params=pltpu.CompilerParams(vmem_limit_bytes=4 * MIB),
        name="finish",
    )(lines, scored)


def on_device(n, hidden, norm_gain, head_weight, targets, counts):
    slots, width = hidden.shape
    block = front(hidden, norm_gain, targets)
    direct, masks = moves(n)
    have = {(0, 0): block}
    for shift, mask in direct:
        have[shift, mask] = move(block, shift, mask, n)
    for by in masks[:-1]:
        for (shift, mask), held in list(have.items()):
            if (shift, mask ^ by) not in have:
                have[shift, mask ^ by] = move(held, 0, by, n)
    beside = fetch(have[direct[1]], head_weight), scored_lanes(counts)
    weight, scored, *blocks = lax.optimization_barrier((*beside, *have.values()))
    near = unpack(blocks, width)
    far = move(near, 0, masks[-1], n)
    owners = tuple(have)
    lines = row_stats(n, owners, near, weight)
    owners = tuple((shift, mask ^ masks[-1]) for shift, mask in owners)
    lines = row_stats(n, owners, far, weight, lines)
    lines = lax.all_to_all(lines, "vocab", 0, 0, tiled=True)
    return finish(lines, scored, slots)


def solution(mesh):
    n = mesh.shape["vocab"]
    in_specs = (
        P(("req", "vocab"), None),
        P(),
        P(None, "vocab"),
        P(("req", "vocab")),
        P(("req", "vocab")),
    )
    out_specs = (P(("req", "vocab")), P(("req", "vocab")))

    def step(*args):
        return on_device(n, *args)

    return jax.shard_map(step, mesh=mesh, in_specs=in_specs, out_specs=out_specs, check_vma=False)
```
